32 devices in a mesh: space: 8 (over z, x), tm: 4 (over y, core).
Axes of the slice: x: 2, y: 2, z: 4, core: 2. Of those that a mesh axis runs over, the one named last changes fastest.
Arguments:
- latents: bfloat16 [4, 16, 120, 384], P('tm', 'space'), may hold values from -6 to 6
- conv_gain: float32 [384], replicated, may hold values from 0.25 to 1.75
- conv_weight: bfloat16 [3, 3, 3, 384, 384], replicated, may hold values from -0.0625 to 0.0625
- conv_bias: float32 [384], replicated, may hold values from -3 to 3
- attn_gain: float32 [384], replicated, may hold values from 0.25 to 1.75
- qkv_weight: bfloat16 [384, 1152], replicated, may hold values from -2 to 2, as said below
- proj_weight: bfloat16 [384, 384], replicated, may hold values from -0.3125 to 0.3125
- proj_bias: float32 [384], replicated, may hold values from -3 to 3
Outputs:
- decoded: float32 [4, 16, 120, 384], P('tm', 'space')
The draws below stay inside these ranges and needn't reach their ends.
Inputs may be any that keep to these rules, and one draw needn't show every extreme that they name: qkv_weight is real-valued with independent entries.
All inputs are finite; a program needn't handle non-finite values.
Results may differ from the reference program's by a relative error of at most 0.0095.
The reference program's roundings to bfloat16 on the way (of `conv_act`, `attn_in` and `mixed`) count: a program that leaves them out, or rounds other values in their place, can miss the bound.
Values may be sent and summed in bfloat16 or wider, within the bound.
A program may use at most 128 MiB of HBM per device.

```python
import jax
import jax.numpy as jnp
from jax import lax

C = 384
W = 120
H = 16
FRAMES = 4


def draw_qkv_weight(key, part):
    key = jax.random.fold_in(key, 7)
    base = jnp.clip(jax.random.normal(key, (C, 3 * C), jnp.float32), -4.0, 4.0)
    leading = 2.0
    column_scale = jnp.concatenate([jnp.full((2 * C,), leading, jnp.float32), jnp.ones((C,), jnp.float32)])
    return (base * column_scale * C ** (-0.5)).astype(jnp.bfloat16)


def block_levels(own_key, shape, pieces, low, high):
    level, own = 1.0, jax.random.fold_in(own_key, 6)
    for axis_at, shards_of in pieces:
        heights = jnp.exp(jax.random.uniform(jax.random.fold_in(own, axis_at), (shards_of,), jnp.float32, low / len(pieces), high / len(pieces)))
        level = level * jnp.repeat(heights, shape[axis_at] // shards_of).reshape([-1 if axis == axis_at else 1 for axis in range(len(shape))])
    return level


def normal_values(stream_key, extent, scale, bound, pieces=(), kind=jnp.bfloat16):
    entries = scale * jax.random.normal(stream_key, extent, jnp.float32)
    if pieces:
        entries = entries * block_levels(stream_key, extent, pieces, -0.22, 0.18)
    return jnp.clip(entries, -bound, bound).astype(kind)


def setup_inputs(seed: int = 0) -> dict:
    key_of = jax.random.split(jax.random.key(seed), 9)
    return {
        "latents": normal_values(key_of[0], (FRAMES, H, W, C), 1.0, 6.0, ((0, 4), (1, 8))),
        "conv_gain": jnp.clip(1.0 + 0.15 * jax.random.normal(key_of[1], (C,), jnp.float32), 0.25, 1.75),
        "conv_weight": normal_values(key_of[2], (3, 3, 3, C, C), (27 * C) ** -0.5, 0.0625),
        "conv_bias": normal_values(key_of[3], (C,), 0.3, 3.0, (), jnp.float32),
        "attn_gain": jnp.clip(1.0 + 0.15 * jax.random.normal(key_of[4], (C,), jnp.float32), 0.25, 1.75),
        "qkv_weight": draw_qkv_weight(jax.random.fold_in(key_of[8], 71), 0),
        "proj_weight": normal_values(key_of[6], (C, C), C ** -0.5, 0.3125),
        "proj_bias": normal_values(key_of[7], (C,), 0.3, 3.0, (), jnp.float32),
    }


def normed(v, gain):
    v = v.astype(jnp.float32)
    return v * lax.rsqrt(lax.optimization_barrier(jnp.mean(v * v, axis=-1, keepdims=True)) + 1e-06) * gain

def causal_conv(act, weight, bias):
    frames, rows, cols, chans = act.shape
    padded = jnp.pad(act, ((2, 0), (1, 1), (1, 1), (0, 0)))
    total = jnp.zeros((frames * rows * cols, weight.shape[4]), jnp.float32)
    for i in range(3):
        for j in range(3):
            for k in range(3):
                window = padded[i:i + frames, j:j + rows, k:k + cols, :].reshape(-1, chans)
                total = total + jnp.dot(window, weight[i, j, k], preferred_element_type=jnp.float32)
    return (total + bias).reshape(frames, rows, cols, -1)

def frame_attention(feature, qkv_weight):
    chans = feature.shape[-1]
    queries = jnp.dot(feature, qkv_weight[:, :chans], preferred_element_type=jnp.float32).astype(jnp.bfloat16)
    keys = jnp.dot(feature, qkv_weight[:, chans:2 * chans], preferred_element_type=jnp.float32).astype(jnp.bfloat16)
    values = jnp.dot(feature, qkv_weight[:, 2 * chans:], preferred_element_type=jnp.float32).astype(jnp.bfloat16)
    blocks = queries.reshape(-1, W, chans)

    def one_block(query_block):
        scores = jnp.dot(query_block, keys.T, preferred_element_type=jnp.float32) * chans ** (-0.5)
        top = lax.optimization_barrier(jnp.max(scores, axis=-1, keepdims=True))
        weights = jnp.exp(scores - top)
        total = lax.optimization_barrier(jnp.sum(weights, axis=-1, keepdims=True))
        mixed = jnp.dot(weights.astype(jnp.bfloat16), values, preferred_element_type=jnp.float32) / total
        return mixed.astype(jnp.bfloat16)
    return lax.map(one_block, blocks).reshape(-1, chans)

def reference(latents, conv_gain, conv_weight, conv_bias, attn_gain, qkv_weight, proj_weight, proj_bias):
    conv_act = jax.nn.silu(normed(latents, conv_gain)).astype(jnp.bfloat16)
    block_out = latents.astype(jnp.float32) + causal_conv(conv_act, conv_weight, conv_bias)
    attn_in = normed(block_out, attn_gain).astype(jnp.bfloat16)
    frames, rows, cols, chans = attn_in.shape
    flat = attn_in.reshape(frames, rows * cols, chans)
    mixed = lax.map(lambda feature: frame_attention(feature, qkv_weight), flat)
    projected = jnp.dot(mixed.reshape(-1, chans), proj_weight, preferred_element_type=jnp.float32) + proj_bias
    decoded = block_out.reshape(-1, chans) + projected
    return decoded.reshape(frames, rows, cols, chans)
```

```python
import functools

import jax
import jax.numpy as jnp
from jax import lax
from jax.experimental import pallas as pl
from jax.experimental.pallas import tpu as pltpu
from jax.sharding import PartitionSpec as P

MESH = pl.DeviceIdType.MESH
F32, BF16 = jnp.float32, jnp.bfloat16


def normed(v, gain):
    return v * lax.rsqrt(jnp.mean(v * v, axis=-1, keepdims=True) + 1e-06) * gain


def dot(a, b):
    return jnp.dot(a, b, preferred_element_type=F32)


def kernel(
    count, frames, padded,
    lat_hbm, cgain, cw_hbm, cbias, again, qkv_hbm, proj_hbm, pbias, out,
    lat, cw, qkv, proj, frame, taps, block, gathered, query, high, denom, accum,
    in_sem, cw_sem, send, recv, up1, dn1, up2, dn2, to_a, to_b, line_sem, b_sem, a_sem, b_dn_sem,
):
    t, s = lax.axis_index("tm"), lax.axis_index("space")
    rows, cols, chans = lat.shape[1:]
    cells = rows * cols
    na = cells - (cells * 2 // 5) // 16 * 16
    nb = cells - na
    hi, lo = lax.div(s, 2), lax.rem(s, 2)
    nhi = count // 2
    mate = s + 1 - 2 * lo
    twin = t + 1 - 2 * lax.rem(t, 2)
    has_up, has_dn = s > 0, s < count - 1
    old = t >= 2
    near = [
        (s >= 1, {"space": s - 1}),
        (s < count - 1, {"space": s + 1}),
        (s >= 2, {"space": s - 2}),
        (s < count - 2, {"space": s + 2}),
        (t >= 2, {"tm": t - 2}),
        (t < frames - 2, {"tm": t + 2}),
        (True, {"tm": twin}),
    ]
    barrier = pltpu.get_barrier_semaphore()
    for there, device in near:
        @pl.when(there)
        def _():
            pl.semaphore_signal(barrier, inc=1, device_id=device, device_id_type=MESH)

    get_lat = pltpu.make_async_copy(lat_hbm, lat, in_sem.at[0])
    get_qkv = pltpu.make_async_copy(qkv_hbm, qkv, in_sem.at[1])
    get_proj = pltpu.make_async_copy(proj_hbm, proj, in_sem.at[2])
    get_cw = [pltpu.make_async_copy(cw_hbm.at[i], cw.at[i], cw_sem.at[i]) for i in range(3)]
    get_lat.start()
    for i in (2, 0, 1):
        get_cw[i].start()
    get_qkv.start()
    get_proj.start()

    def zero_row(f, r):
        frame[f, r] = jnp.zeros((padded, chans), BF16)

    @pl.when(s == 0)
    def _():
        zero_row(2, 0)
        zero_row(0, 0)

    @pl.when(s == count - 1)
    def _():
        zero_row(2, rows + 1)
        zero_row(0, rows + 1)

    get_lat.wait()
    for r in range(rows):
        act = jax.nn.silu(normed(lat[0, r].astype(F32), cgain[...]))
        act = jnp.concatenate([act, jnp.zeros((padded - cols, chans), F32)], axis=0)
        frame[2, r + 1] = act.astype(BF16)

    pl.semaphore_wait(barrier, sum(there.astype(jnp.int32) for there, _ in near[:-1]) + 1)

    def remote(src, dst, ssem, rsem, device):
        return pltpu.make_async_remote_copy(
            src_ref=src, dst_ref=dst, send_sem=ssem, recv_sem=rsem,
            device_id=device, device_id_type=MESH,
        )

    body = pl.ds(1, rows)
    later = remote(frame.at[2, body], frame.at[0, body], send.at[0], recv.at[0], {"tm": t + 2})
    own_up = remote(frame.at[2, 1], frame.at[2, rows + 1], send.at[1], recv.at[1], {"space": s - 1})
    own_dn = remote(frame.at[2, rows], frame.at[2, 0], send.at[2], recv.at[2], {"space": s + 1})
    old_up = remote(frame.at[0, 1], frame.at[0, rows + 1], send.at[3], recv.at[3], {"space": s - 1})
    old_dn = remote(frame.at[0, rows], frame.at[0, 0], send.at[4], recv.at[4], {"space": s + 1})
    twin_own = remote(frame.at[2], frame.at[1], send.at[5], recv.at[5], {"tm": twin})
    twin_old = remote(frame.at[0], frame.at[1], send.at[5], recv.at[5], {"tm": twin})
    is_even = lax.rem(t, 2) == 0
    gives_old = jnp.logical_and(t >= 3, jnp.logical_not(is_even))

    pl.when(t < frames - 2)(later.start)
    pl.when(has_up)(own_up.start)
    pl.when(has_dn)(own_dn.start)

    @pl.when(old)
    def _():
        later.wait_recv()
        pl.when(has_up)(old_up.start)
        pl.when(has_dn)(old_dn.start)

    pl.when(has_dn)(own_up.wait_recv)
    pl.when(has_up)(own_dn.wait_recv)
    pl.when(is_even)(twin_own.start)

    def conv_step(i, first):
        left = jnp.concatenate(
            [frame[i, pl.ds(j, rows)].reshape(rows * padded, chans) for j in range(3)], axis=1
        )
        for k in range(3):
            right = jnp.concatenate([cw[i, j, k] for j in range(3)], axis=0)
            part = dot(left, right)
            taps[k] = part if first else taps[k] + part

    get_cw[2].wait()
    conv_step(2, True)
    get_cw[0].wait()

    @pl.when(old)
    def _():
        pl.when(has_dn)(old_up.wait_recv)
        pl.when(has_up)(old_dn.wait_recv)
        pl.when(gives_old)(twin_old.start)
        conv_step(0, False)

    get_cw[1].wait()

    @pl.when(t >= 1)
    def _():
        twin_own.wait_recv()
        conv_step(1, False)

    for r in range(rows):
        at = pl.ds(r * padded, padded)
        sums = pltpu.roll(taps[0, at], 1, 0) + taps[1, at] + pltpu.roll(taps[2, at], padded - 1, 0)
        sums = sums[:cols] + cbias[...]
        block[pl.ds(r * cols, cols)] = lat[0, r].astype(F32) + sums
    attn_in = normed(block[...], again[...]).astype(BF16)
    gathered[s] = attn_in

    part_a, part_b = pl.ds(0, na), pl.ds(na, nb)

    def line(sems, rsems, h, lane, step, part=None):
        ref = gathered.at[2 * h + lane]
        ref = ref if part is None else gathered.at[2 * h + lane, part]
        return remote(ref, ref, sems.at[h], rsems.at[h], {"space": s + 2 * step})

    def full_up(h):
        return line(up1, line_sem, h, lo, 1)

    def full_dn(h):
        return line(dn1, line_sem, h, lo, -1)

    def b_up(h):
        return line(up2, b_sem, h, 1 - lo, 1, part_b)

    def b_dn(h):
        return line(dn2, b_sem, h, 1 - lo, -1, part_b)

    def a_over(h, mine):
        ref = gathered.at[2 * h + jnp.where(mine, lo, 1 - lo), part_a]
        return remote(ref, ref, to_a.at[h], a_sem.at[h], {"space": mate})

    def b_over(mine):
        ref = gathered.at[2 * hi + jnp.where(mine, lo, 1 - lo), part_b]
        return remote(ref, ref, to_b.at[0], b_dn_sem.at[0], {"space": mate})

    above, below = hi < nhi - 1, hi > 0
    b_over(True).start()
    pl.when(above)(full_up(hi).start)
    pl.when(below)(full_dn(hi).start)
    a_over(hi, True).start()

    get_qkv.wait()
    get_proj.wait()
    query[...] = dot(attn_in, qkv[:, :chans]).astype(BF16)
    high[...] = jnp.full(high.shape, -jnp.inf, F32)
    denom[...] = jnp.zeros(denom.shape, F32)
    accum[...] = jnp.zeros(accum.shape, F32)

    b_over(False).wait_recv()
    pl.when(above)(b_up(hi).start)
    pl.when(below)(b_dn(hi).start)
    a_over(hi, False).wait_recv()

    def attend(h):
        feats = gathered[pl.ds(2 * h, 2)].reshape(2 * cells, chans)
        keys = dot(feats, qkv[:, chans : 2 * chans]).astype(BF16)
        values = dot(feats, qkv[:, 2 * chans :]).astype(BF16)
        scores = lax.dot_general(
            query[...], keys, (((1,), (1,)), ((), ())), preferred_element_type=F32
        ) * (chans ** -0.5)
        top = jnp.maximum(high[...], jnp.max(scores, axis=-1, keepdims=True))
        factor = jnp.exp(high[...] - top)
        weights = jnp.exp(scores - top)
        high[...] = top
        denom[...] = denom[...] * factor + jnp.sum(weights, axis=-1, keepdims=True)
        accum[...] = accum[...] * factor + dot(weights.astype(BF16), values)

    attend(hi)

    def arrive(h, here, onward, first, second):
        @pl.when(here)
        def _():
            first(h).wait_recv()
            pl.when(onward)(first(h).start)
            a_over(h, True).start()

    def arrive_b(h, here, onward, second):
        @pl.when(here)
        def _():
            second(h).wait_recv()
            pl.when(onward)(second(h).start)

    def finish(h, here):
        @pl.when(here)
        def _():
            a_over(h, False).wait_recv()
            attend(h)

    def step(d, carry):
        from_below, from_above = hi - d, hi + d
        low_here, up_here = from_below >= 0, from_above < nhi
        arrive(from_below, low_here, above, full_up, b_up)
        arrive(from_above, up_here, below, full_dn, b_dn)
        arrive_b(from_below, low_here, above, b_up)
        arrive_b(from_above, up_here, below, b_dn)
        finish(from_below, low_here)
        finish(from_above, up_here)
        return carry

    lax.fori_loop(1, nhi, step, 0)

    mixed = (accum[...] / denom[...]).astype(BF16)
    decoded = block[...] + (dot(mixed, proj[...]) + pbias[...])
    for r in range(rows):
        out[0, r] = decoded[r * cols : (r + 1) * cols]

    pl.when(t < frames - 2)(later.wait_send)
    pl.when(has_up)(own_up.wait_send)
    pl.when(has_dn)(own_dn.wait_send)
    pl.when(jnp.logical_and(old, has_up))(old_up.wait_send)
    pl.when(jnp.logical_and(old, has_dn))(old_dn.wait_send)
    pl.when(is_even)(twin_own.wait_send)
    pl.when(gives_old)(twin_old.wait_send)
    b_over(True).wait_send()

    def drain(h, carry):
        a_over(h, True).wait_send()

        @pl.when(jnp.logical_and(h <= hi, above))
        def _():
            full_up(h).wait_send()
            b_up(h).wait_send()

        @pl.when(jnp.logical_and(h >= hi, below))
        def _():
            full_dn(h).wait_send()
            b_dn(h).wait_send()

        return carry

    lax.fori_loop(0, nhi, drain, 0)


def solution(mesh):
    count, frames = mesh.shape["space"], mesh.shape["tm"]

    def on_device(
        latents, conv_gain, conv_weight, conv_bias, attn_gain, qkv_weight, proj_weight, proj_bias
    ):
        _, rows, cols, chans = latents.shape
        padded = (cols + 16) // 16 * 16
        cells = rows * cols
        nhi = count // 2
        anywhere = pl.BlockSpec(memory_space=pl.ANY)
        local = pl.BlockSpec(memory_space=pltpu.VMEM)
        dma = pltpu.SemaphoreType.DMA
        return pl.pallas_call(
            functools.partial(kernel, count, frames, padded),
            out_shape=jax.ShapeDtypeStruct(latents.shape, F32),
            in_specs=[anywhere, local, anywhere, local, local, anywhere, anywhere, local],
            out_specs=local,
            scratch_shapes=[
                pltpu.VMEM(latents.shape, BF16),
                pltpu.VMEM(conv_weight.shape, BF16),
                pltpu.VMEM(qkv_weight.shape, BF16),
                pltpu.VMEM(proj_weight.shape, BF16),
                pltpu.VMEM((3, rows + 2, padded, chans), BF16),
                pltpu.VMEM((3, rows * padded, chans), F32),
                pltpu.VMEM((cells, chans), F32),
                pltpu.VMEM((count, cells, chans), BF16),
                pltpu.VMEM((cells, chans), BF16),
                pltpu.VMEM((cells, 1), F32),
                pltpu.VMEM((cells, 1), F32),
                pltpu.VMEM((cells, chans), F32),
                dma((3,)), dma((3,)), dma((6,)), dma((6,)),
                dma((nhi,)), dma((nhi,)), dma((nhi,)), dma((nhi,)), dma((nhi,)), dma((1,)),
                dma((nhi,)), dma((nhi,)), dma((nhi,)), dma((1,)),
            ],
            compiler_params=pltpu.CompilerParams(
                collective_id=0, has_side_effects=True, vmem_limit_bytes=48 * 2**20
            ),
        )(
            latents, conv_gain.reshape(1, chans), conv_weight, conv_bias.reshape(1, chans),
            attn_gain.reshape(1, chans), qkv_weight, proj_weight, proj_bias.reshape(1, chans),
        )

    in_specs = (P("tm", "space", None, None), P(), P(), P(), P(), P(), P(), P())
    return jax.shard_map(
        on_device, mesh=mesh, in_specs=in_specs,
        out_specs=P("tm", "space", None, None), check_vma=False,
    )
```

```python
import functools

import jax
import jax.numpy as jnp
from jax import lax
from jax.experimental import pallas as pl
from jax.experimental.pallas import tpu as pltpu
from jax.sharding import PartitionSpec as P

MESH = pl.DeviceIdType.MESH
F32, BF16 = jnp.float32, jnp.bfloat16
MATE_DIRECT, FAR_DIRECT = False, False
CHUNKS, CROSS_FIRST = (5, 3, 2), 1


def normed(v, gain):
    return v * lax.rsqrt(jnp.mean(v * v, axis=-1, keepdims=True) + 1e-06) * gain


def dot(a, b):
    return jnp.dot(a, b, preferred_element_type=F32)


def kernel(
    count, frames, padded, chunks,
    lat_hbm, cgain_hbm, cw_hbm, cbias_hbm, again_hbm, qkv_hbm, proj_hbm, pbias_hbm, out,
    lat, cgain, cbias, again, pbias, cw, qkv, proj, frame, taps, block, gathered, query, high, denom, accum,
    in_sem, vec_sem, cw_sem, later_send, later_recv, send, recv, up1, dn1, up2, dn2, to_a, line_sem, b_sem, a_sem,
):
    t, s = lax.axis_index("tm"), lax.axis_index("space")
    rows, cols, chans = lat.shape[1:]
    cells = rows * cols
    size = cells // chunks
    na = chunks - CROSS_FIRST
    early = chunks
    hi, lo = lax.div(s, 2), lax.rem(s, 2)
    nhi = count // 2
    mate = s + 1 - 2 * lo
    twin = t + 1 - 2 * lax.rem(t, 2)
    old = t >= 2
    near = [
        (s >= 1, {"space": s - 1}),
        (s < count - 1, {"space": s + 1}),
        (s >= 2, {"space": s - 2}),
        (s < count - 2, {"space": s + 2}),
        (t >= 2, {"tm": t - 2}),
        (t < frames - 2, {"tm": t + 2}),
        (True, {"tm": twin}),
    ]
    barrier = pltpu.get_barrier_semaphore()
    for there, device in near:
        @pl.when(there)
        def _():
            pl.semaphore_signal(barrier, inc=1, device_id=device, device_id_type=MESH)

    get_lat = pltpu.make_async_copy(lat_hbm, lat, in_sem.at[0])
    get_qkv = pltpu.make_async_copy(qkv_hbm, qkv, in_sem.at[1])
    get_proj = pltpu.make_async_copy(proj_hbm, proj, in_sem.at[2])
    get_cw = [pltpu.make_async_copy(cw_hbm.at[i], cw.at[i], cw_sem.at[i]) for i in range(3)]
    pairs = [(cgain_hbm, cgain), (cbias_hbm, cbias), (again_hbm, again), (pbias_hbm, pbias)]
    get_vec = [pltpu.make_async_copy(a, b, vec_sem.at[i]) for i, (a, b) in enumerate(pairs)]
    get_lat.start()
    for copy in get_vec:
        copy.start()
    for i in (2, 0, 1):
        get_cw[i].start()
    get_qkv.start()
    get_proj.start()

    def zero_row(f, r):
        frame[f, r] = jnp.zeros((padded, chans), BF16)

    @pl.when(s == 0)
    def _():
        zero_row(2, 0)
        zero_row(0, 0)

    @pl.when(s == count - 1)
    def _():
        zero_row(2, rows + 1)
        zero_row(0, rows + 1)

    get_lat.wait()
    get_vec[0].wait()
    for r in range(rows):
        act = jax.nn.silu(normed(lat[0, r].astype(F32), cgain[...][None]))
        act = jnp.concatenate([act, jnp.zeros((padded - cols, chans), F32)], axis=0)
        frame[2, r + 1] = act.astype(BF16)

    pl.semaphore_wait(barrier, sum(there.astype(jnp.int32) for there, _ in near[:-1]) + 1)

    def remote(src, dst, ssem, rsem, device):
        return pltpu.make_async_remote_copy(
            src_ref=src, dst_ref=dst, send_sem=ssem, recv_sem=rsem,
            device_id=device, device_id_type=MESH,
        )

    far = s - 1 + 2 * lo
    far_here = jnp.logical_and(far >= 0, far < count)
    mate_src, mate_dst = jnp.where(lo == 0, rows, 1), jnp.where(lo == 0, 0, rows + 1)
    far_src, far_dst = jnp.where(lo == 0, 1, rows), jnp.where(lo == 0, rows + 1, 0)
    mate_land, far_land = rows + 1 - mate_dst, rows + 1 - far_dst
    onward = t < frames - 2

    later = [
        remote(frame.at[2, r], frame.at[0, r], later_send.at[r - 1], later_recv.at[r - 1], {"tm": t + 2})
        for r in range(1, rows + 1)
    ]

    def edge(src, f, to_mate, k, device):
        at, to = (mate_src, mate_dst) if to_mate else (far_src, far_dst)
        return remote(frame.at[src, at], frame.at[f, to], send.at[k], recv.at[k], device)

    def landing(f, of_mate, k):
        ref = frame.at[f, mate_land if of_mate else far_land]
        return remote(ref, ref, send.at[k], recv.at[k], {"space": mate})

    own_mate = edge(2, 2, True, 0, {"space": mate})
    own_far = edge(2, 2, False, 1, {"space": far})
    if MATE_DIRECT:
        old_mate, gives_mate = edge(2, 0, True, 2, {"space": mate, "tm": t + 2}), onward
    else:
        old_mate, gives_mate = edge(0, 0, True, 2, {"space": mate}), old
    if FAR_DIRECT:
        old_far, gives_far = edge(2, 0, False, 3, {"space": far, "tm": t + 2}), jnp.logical_and(far_here, onward)
    else:
        old_far, gives_far = edge(0, 0, False, 3, {"space": far}), jnp.logical_and(far_here, old)
    twin_own = remote(frame.at[2], frame.at[1], send.at[4], recv.at[4], {"tm": twin})
    twin_old = remote(frame.at[0], frame.at[1], send.at[4], recv.at[4], {"tm": twin})
    is_even = lax.rem(t, 2) == 0
    gives_old = jnp.logical_and(t >= 3, jnp.logical_not(is_even))

    pl.when(far_here)(own_far.start)
    own_mate.start()

    @pl.when(onward)
    def _():
        for copy in later:
            copy.start()

    if FAR_DIRECT:
        pl.when(gives_far)(old_far.start)
    if MATE_DIRECT:
        pl.when(gives_mate)(old_mate.start)

    @pl.when(old)
    def _():
        for copy in later:
            copy.wait_recv()
        if not FAR_DIRECT:
            pl.when(far_here)(old_far.start)
        if not MATE_DIRECT:
            old_mate.start()

    landing(2, True, 0).wait_recv()
    pl.when(far_here)(landing(2, False, 1).wait_recv)
    pl.when(is_even)(twin_own.start)

    def conv_step(i, first):
        left = jnp.concatenate(
            [frame[i, pl.ds(j, rows)].reshape(rows * padded, chans) for j in range(3)], axis=1
        )
        for k in range(3):
            right = jnp.concatenate([cw[i, j, k] for j in range(3)], axis=0)
            part = dot(left, right)
            taps[k] = part if first else taps[k] + part

    get_cw[2].wait()
    conv_step(2, True)
    get_cw[0].wait()

    @pl.when(old)
    def _():
        landing(0, True, 2).wait_recv()
        pl.when(far_here)(landing(0, False, 3).wait_recv)
        pl.when(gives_old)(twin_old.start)
        conv_step(0, False)

    get_cw[1].wait()

    @pl.when(t >= 1)
    def _():
        twin_own.wait_recv()
        conv_step(1, False)

    for copy in get_vec[1:]:
        copy.wait()
    for r in range(rows):
        at = pl.ds(r * padded, padded)
        sums = pltpu.roll(taps[0, at], 1, 0) + taps[1, at] + pltpu.roll(taps[2, at], padded - 1, 0)
        sums = sums[:cols] + cbias[...][None]
        block[pl.ds(r * cols, cols)] = lat[0, r].astype(F32) + sums
    attn_in = normed(block[...], again[...][None]).astype(BF16)
    gathered[s] = attn_in

    def part(h, lane, c):
        return gathered.at[2 * h + lane, pl.ds(c * size, size)]

    def along(h, c, step):
        sems = up1 if step > 0 else dn1
        ref = part(h, lo, c)
        return remote(ref, ref, sems.at[h, c], line_sem.at[h, c], {"space": s + 2 * step})

    def along_b(h, c, step):
        sems = up2 if step > 0 else dn2
        ref = part(h, 1 - lo, c)
        return remote(ref, ref, sems.at[h, c - na], b_sem.at[h, c - na], {"space": s + 2 * step})

    def over(h, c, mine=True):
        ref = part(h, lo if mine else 1 - lo, c)
        return remote(ref, ref, to_a.at[h, c], a_sem.at[h, c], {"space": mate})

    above, below = hi < nhi - 1, hi > 0
    for c in range(na, chunks):
        over(hi, c).start()
    for c in range(chunks):
        pl.when(above)(along(hi, c, 1).start)
        pl.when(below)(along(hi, c, -1).start)
        if c < na:
            over(hi, c).start()

    get_qkv.wait()
    get_proj.wait()
    query[...] = dot(attn_in, qkv[:, :chans]).astype(BF16)
    high[...] = jnp.full(high.shape, -jnp.inf, F32)
    denom[...] = jnp.zeros(denom.shape, F32)
    accum[...] = jnp.zeros(accum.shape, F32)

    for c in range(na, chunks):
        over(hi, c, False).wait_recv()
        pl.when(above)(along_b(hi, c, 1).start)
        pl.when(below)(along_b(hi, c, -1).start)

    def attend(h):
        feats = gathered[pl.ds(2 * h, 2)].reshape(2 * cells, chans)
        keys = dot(feats, qkv[:, chans : 2 * chans]).astype(BF16)
        values = dot(feats, qkv[:, 2 * chans :]).astype(BF16)
        scores = lax.dot_general(
            query[...], keys, (((1,), (1,)), ((), ())), preferred_element_type=F32
        ) * (chans ** -0.5)
        top = jnp.maximum(high[...], jnp.max(scores, axis=-1, keepdims=True))
        factor = jnp.exp(high[...] - top)
        weights = jnp.exp(scores - top)
        high[...] = top
        denom[...] = denom[...] * factor + jnp.sum(weights, axis=-1, keepdims=True)
        accum[...] = accum[...] * factor + dot(weights.astype(BF16), values)

    def arrive(h, c, here, onward, direction):
        @pl.when(here)
        def _():
            along(h, c, direction).wait_recv()
            pl.when(onward)(along(h, c, direction).start)
            if c < na:
                over(h, c).start()

    def arrive_b(h, c, here, onward, direction):
        @pl.when(here)
        def _():
            along_b(h, c, direction).wait_recv()
            pl.when(onward)(along_b(h, c, direction).start)

    def finish(h, here):
        @pl.when(here)
        def _():
            for c in range(na):
                over(h, c, False).wait_recv()
            attend(h)

    def finish_own():
        for c in range(na):
            over(hi, c, False).wait_recv()
        attend(hi)

    def arrivals(d, some):
        for c in some:
            arrive(hi - d, c, hi - d >= 0, above, 1)
            arrive(hi + d, c, hi + d < nhi, below, -1)

    def step(d, carry):
        arrivals(d, range(early))
        for c in range(na, chunks):
            arrive_b(hi - d, c, hi - d >= 0, above, 1)
            arrive_b(hi + d, c, hi + d < nhi, below, -1)

        @pl.when(d == 1)
        def _():
            finish_own()

        @pl.when(d > 1)
        def _():
            finish(hi - d + 1, hi - d + 1 >= 0)
            finish(hi + d - 1, hi + d - 1 < nhi)

        arrivals(d, range(early, chunks))
        return carry

    lax.fori_loop(1, nhi, step, 0)
    finish(hi - nhi + 1, hi - nhi + 1 >= 0)
    finish(hi + nhi - 1, hi + nhi - 1 < nhi)

    mixed = (accum[...] / denom[...]).astype(BF16)
    decoded = block[...] + (dot(mixed, proj[...]) + pbias[...][None])
    for r in range(rows):
        out[0, r] = decoded[r * cols : (r + 1) * cols]

    @pl.when(onward)
    def _():
        for copy in later:
            copy.wait_send()

    own_mate.wait_send()
    pl.when(far_here)(own_far.wait_send)
    pl.when(gives_mate)(old_mate.wait_send)
    pl.when(gives_far)(old_far.wait_send)
    pl.when(is_even)(twin_own.wait_send)
    pl.when(gives_old)(twin_old.wait_send)

    def drain(h, carry):
        for c in range(na):
            over(h, c).wait_send()

        @pl.when(jnp.logical_and(h <= hi, above))
        def _():
            for c in range(chunks):
                along(h, c, 1).wait_send()
            for c in range(na, chunks):
                along_b(h, c, 1).wait_send()

        @pl.when(jnp.logical_and(h >= hi, below))
        def _():
            for c in range(chunks):
                along(h, c, -1).wait_send()
            for c in range(na, chunks):
                along_b(h, c, -1).wait_send()

        return carry

    lax.fori_loop(0, nhi, drain, 0)
    for c in range(na, chunks):
        over(hi, c).wait_send()


def solution(mesh):
    count, frames = mesh.shape["space"], mesh.shape["tm"]

    def on_device(
        latents, conv_gain, conv_weight, conv_bias, attn_gain, qkv_weight, proj_weight, proj_bias
    ):
        _, rows, cols, chans = latents.shape
        padded = (cols + 16) // 16 * 16
        cells = rows * cols
        nhi = count // 2
        chunks = next(n for n in CHUNKS if cells % (16 * n) == 0)
        anywhere = pl.BlockSpec(memory_space=pltpu.HBM)
        local = pl.BlockSpec(memory_space=pltpu.VMEM)
        dma = pltpu.SemaphoreType.DMA
        return pl.pallas_call(
            functools.partial(kernel, count, frames, padded, chunks),
            out_shape=jax.ShapeDtypeStruct(latents.shape, F32),
            in_specs=[anywhere] * 8,
            out_specs=local,
            scratch_shapes=[
                pltpu.VMEM(latents.shape, BF16),
                *[pltpu.VMEM((chans,), F32)] * 4,
                pltpu.VMEM(conv_weight.shape, BF16),
                pltpu.VMEM(qkv_weight.shape, BF16),
                pltpu.VMEM(proj_weight.shape, BF16),
                pltpu.VMEM((3, rows + 2, padded, chans), BF16),
                pltpu.VMEM((3, rows * padded, chans), F32),
                pltpu.VMEM((cells, chans), F32),
                pltpu.VMEM((count, cells, chans), BF16),
                pltpu.VMEM((cells, chans), BF16),
                pltpu.VMEM((cells, 1), F32),
                pltpu.VMEM((cells, 1), F32),
                pltpu.VMEM((cells, chans), F32),
                dma((3,)), dma((4,)), dma((3,)), dma((rows,)), dma((rows,)), dma((5,)), dma((5,)),
                dma((nhi, chunks)), dma((nhi, chunks)), dma((nhi, CROSS_FIRST)), dma((nhi, CROSS_FIRST)),
                dma((nhi, chunks)), dma((nhi, chunks)), dma((nhi, CROSS_FIRST)), dma((nhi, chunks)),
            ],
            compiler_params=pltpu.CompilerParams(
                collective_id=0, has_side_effects=True, vmem_limit_bytes=60 * 2**20
            ),
        )(
            latents, conv_gain, conv_weight, conv_bias,
            attn_gain, qkv_weight, proj_weight, proj_bias,
        )

    in_specs = (P("tm", "space", None, None), P(), P(), P(), P(), P(), P(), P())
    return jax.shard_map(
        on_device, mesh=mesh, in_specs=in_specs,
        out_specs=P("tm", "space", None, None), check_vma=False,
    )
```
